32 devices in a mesh: tm: 4 (over z), rows: 8 (over y, x, core).
Axes of the slice: x: 2, y: 2, z: 4, core: 2. Of those that a mesh axis runs over, the one named last changes fastest.
Arguments:
- video: bfloat16 [1, 16, 64, 128, 256], P(None, 'tm', 'rows'), may hold values from -6 to 6
- spatial_weight: bfloat16 [2304, 256], P(('tm', 'rows')), may hold values from -0.125 to 0.125
- temporal_weight: bfloat16 [768, 256], P(('tm', 'rows')), may hold values from -0.21875 to 0.21875
- cotangent: bfloat16 [1, 16, 64, 128, 256], P(None, 'tm', 'rows'), may hold values from -6 to 6
Outputs:
- output: bfloat16 [1, 16, 64, 128, 256], P(None, 'tm', 'rows')
- grad_video: bfloat16 [1, 16, 64, 128, 256], P(None, 'tm', 'rows')
- grad_spatial: float32 [2304, 256], P(('tm', 'rows'))
- grad_temporal: float32 [768, 256], P(('tm', 'rows'))
The draws below stay inside these ranges and needn't reach their ends.
All inputs are finite; a program needn't handle non-finite values.
Results may differ from the reference program's by a relative error of at most 0.0053.
Values may be sent and summed in bfloat16 or wider, within the bound.
A program may use at most 128 MiB of HBM per device.

```python
import jax
import jax.numpy as jnp
from jax import lax

C = 256
BATCH = 1
COLS = 128
FRAMES = 16
HEIGHT = 64


def spiked(drawn, stream_key, source, target, parts, factor):
    def block_of(axis_at):
        return (jnp.arange(drawn.shape[axis_at]) // (drawn.shape[axis_at] // parts)).reshape((-1,) + (1,) * (drawn.ndim - 1 - axis_at))

    one_side = jax.random.permutation(stream_key, parts)[block_of(target)]
    far = (block_of(target) + parts // 2) % parts
    return jnp.where((block_of(source) == one_side) | (block_of(source) == far), factor * drawn, drawn)


def steps_of(key, shape, cuts, low, largest):
    level = 1.0
    for axis_at, parts in cuts:
        heights = jax.random.uniform(jax.random.fold_in(jax.random.fold_in(key, 6), axis_at), (parts,), jnp.float32, low / len(cuts), largest / len(cuts))
        level = level * jnp.repeat(jnp.exp(heights), shape[axis_at] // parts).reshape((-1,) + (1,) * (len(shape) - 1 - axis_at))
    return level


def gaussian(rng, dims, scale, reach, cuts=(), kind=jnp.bfloat16):
    gain = steps_of(rng, dims, cuts, -0.22, 0.18) if cuts else 1.0
    values = jax.random.normal(rng, dims, jnp.float32) * scale * gain
    return jnp.minimum(jnp.maximum(values, -reach), reach).astype(kind)


def bell_draw_with(stream_key, shape, scale, bound, cuts, heavy, kind=jnp.bfloat16):
    array = scale * jax.random.normal(stream_key, shape, jnp.float32)
    if cuts:
        array = array * steps_of(stream_key, shape, cuts, -0.22, 0.18)
    return jnp.clip(spiked(array, jax.random.fold_in(stream_key, 3), *heavy), -bound, bound).astype(kind)


def setup_inputs(seed: int = 0) -> dict:
    arg_keys = jax.random.split(jax.random.key(seed), 5)
    video = gaussian(arg_keys[0], (BATCH, FRAMES, HEIGHT, COLS, C), 1.0, 6.0, ((1, 4), (2, 8)))
    spatial_weight = gaussian(arg_keys[1], (9 * C, C), (9 * C) ** -0.5, 0.125, ((0, 32),))
    temporal_weight = gaussian(arg_keys[2], (3 * C, C), (3 * C) ** -0.5, 0.21875, ((0, 32),))
    cotangent = bell_draw_with(arg_keys[3], (BATCH, FRAMES, HEIGHT, COLS, C), 1.0, 6.0, ((1, 4), (2, 8)), (2, 4, 8, 2.0))
    return dict(video=video, spatial_weight=spatial_weight, temporal_weight=temporal_weight, cotangent=cotangent)


epsilon = 1e-06

def spatial_cols(field):
    padded = jnp.pad(field, ((1, 1), (1, 1), (0, 0)))
    n_rows, n_cols = (field.shape[0], field.shape[1])
    pieces = [padded[i:i + n_rows, j:j + n_cols] for i in range(3) for j in range(3)]
    return jnp.concatenate(pieces, axis=-1).reshape(n_rows * n_cols, -1)

def silu_slope(value):
    sigmoid = jax.nn.sigmoid(value)
    return sigmoid * (1.0 + value * (1.0 - sigmoid))

def contract(left, right):
    return lax.dot_general(left, right, (((0,), (0,)), ((), ())), preferred_element_type=jnp.float32)

def normalize(one_frame):
    values = one_frame.astype(jnp.float32)
    inv_rms = lax.rsqrt(lax.optimization_barrier(jnp.mean(values * values, axis=-1, keepdims=True)) + epsilon)
    return (values * inv_rms, inv_rms)

def reverse_spatial(weight, chans):
    return weight.reshape(3, 3, chans, chans)[::-1, ::-1].transpose(0, 1, 3, 2).reshape(9 * chans, chans)

def reverse_temporal(weight, chans):
    return weight.reshape(3, chans, chans)[::-1].transpose(0, 2, 1).reshape(3 * chans, chans)

def reference(video, spatial_weight, temporal_weight, cotangent):
    n_batch, n_frames, n_rows, n_cols, chans = video.shape
    flat_video = video.reshape(n_batch * n_frames, n_rows, n_cols, chans)

    def forward_frame(one_frame):
        normed, inv_rms = normalize(one_frame)
        activated = jax.nn.silu(normed).astype(jnp.bfloat16)
        pre_act = jnp.dot(spatial_cols(activated), spatial_weight, preferred_element_type=jnp.float32)
        return (activated, pre_act.reshape(n_rows, n_cols, chans))
    activated, pre_act = lax.map(forward_frame, flat_video)
    hidden = jax.nn.silu(pre_act).astype(jnp.bfloat16).reshape(n_batch, n_frames, n_rows, n_cols, chans)
    blank = jnp.zeros((n_batch, 2, n_rows, n_cols, chans), jnp.bfloat16)
    past = jnp.concatenate([blank, hidden], axis=1)
    ahead = jnp.concatenate([cotangent, blank], axis=1)
    back_temporal = reverse_temporal(temporal_weight, chans)

    def temporal_frame(carry, frame_idx):
        from_past = jnp.concatenate([lax.dynamic_index_in_dim(past, frame_idx + k, 1, keepdims=False) for k in range(3)], axis=-1).reshape(-1, 3 * chans)
        from_ahead = jnp.concatenate([lax.dynamic_index_in_dim(ahead, frame_idx + k, 1, keepdims=False) for k in range(3)], axis=-1).reshape(-1, 3 * chans)
        grad_out = lax.dynamic_index_in_dim(cotangent, frame_idx, 1, keepdims=False).reshape(-1, chans)
        mixed = jnp.dot(from_past, temporal_weight, preferred_element_type=jnp.float32)
        back = jnp.dot(from_ahead, back_temporal, preferred_element_type=jnp.float32)
        return (carry + contract(from_past, grad_out), (mixed, back))
    grad_temporal, (mixed, back) = lax.scan(temporal_frame, jnp.zeros((3 * chans, chans), jnp.float32), jnp.arange(n_frames, dtype=jnp.int32))
    mixed = mixed.reshape(n_frames, n_batch, n_rows, n_cols, chans).transpose(1, 0, 2, 3, 4)
    back = back.reshape(n_frames, n_batch, n_rows, n_cols, chans).transpose(1, 0, 2, 3, 4)
    output = (video.astype(jnp.float32) + mixed).astype(jnp.bfloat16)
    grad_pre = (back.reshape(n_batch * n_frames, n_rows, n_cols, chans) * silu_slope(pre_act)).astype(jnp.bfloat16)
    back_spatial = reverse_spatial(spatial_weight, chans)
    flat_grad = cotangent.reshape(n_batch * n_frames, n_rows, n_cols, chans)

    def spatial_back(carry, items):
        one_frame, act_frame, pre_grad, grad_frame = items
        normed, inv_rms = normalize(one_frame)
        grad_act = jnp.dot(spatial_cols(pre_grad), back_spatial, preferred_element_type=jnp.float32).reshape(n_rows, n_cols, chans)
        grad_norm = grad_act * silu_slope(normed)
        grad_in = inv_rms * (grad_norm - normed * lax.optimization_barrier(jnp.mean(grad_norm * normed, axis=-1, keepdims=True)))
        result = (grad_frame.astype(jnp.float32) + grad_in).astype(jnp.bfloat16)
        return (carry + contract(spatial_cols(act_frame), pre_grad.reshape(-1, chans)), result)
    grad_spatial, grad_video = lax.scan(spatial_back, jnp.zeros((9 * chans, chans), jnp.float32), (flat_video, activated, grad_pre, flat_grad))
    factor = float(n_batch * n_frames * n_rows * n_cols) ** (-0.5)
    grad_video = grad_video.reshape(n_batch, n_frames, n_rows, n_cols, chans)
    return (output, grad_video, grad_spatial * factor, grad_temporal * factor)
```

```python
import functools

import jax
import jax.numpy as jnp
from jax import lax
from jax.experimental import pallas as pl
from jax.experimental.pallas import tpu as pltpu
from jax.sharding import PartitionSpec as P

epsilon = 1e-06
MESH = pl.DeviceIdType.MESH
f32 = jnp.float32
bf16 = jnp.bfloat16


def mm(a, b):
    return lax.dot_general(a, b, (((1,), (0,)), ((), ())), preferred_element_type=f32)


def silu_slope(value):
    sigmoid = jax.nn.sigmoid(value)
    return sigmoid * (1.0 + value * (1.0 - sigmoid))


def normalize(values):
    inv_rms = lax.rsqrt(jnp.mean(values * values, axis=-1, keepdims=True) + epsilon)
    return values * inv_rms, inv_rms


def kernel(
    dims, video, shard, cot_hbm, output, grad_video, grads,
    wide, act_t, slope, hid, hid_t, cot, acc_s, acc_t, work, w_s, w_t, wb_s, wb_t, gather,
    edge_out, edge_in, rs_out, rs_in, z_out, z_in,
    ag_z_send, ag_z_recv, ag_send, ag_recv, edge_send, edge_recv, frame_send, frame_recv,
    rs_send, rs_recv, z_send, z_recv, cot_sem,
):
    n_t, n_r, F, R, W, C, n_s, n_tmp, factor = dims
    n_bits = n_r.bit_length() - 1
    SH = shard.shape[0]
    half = SH // 2
    CH = 4 if R % 4 == 0 else 1
    per = R // CH
    t, r = lax.axis_index("tm"), lax.axis_index("rows")
    bit = [lax.rem(lax.div(r, 1 << b), 2) for b in range(n_bits)]
    partner = [r + (1 - 2 * bit[b]) * (1 << b) for b in range(n_bits)]

    barrier = pltpu.get_barrier_semaphore()
    peers = [(lax.rem(t + k, n_t), r) for k in range(1, n_t)]
    peers += [(t, partner[b]) for b in range(n_bits)]
    peers += [(t, lax.rem(r + 1, n_r)), (t, lax.rem(r + n_r - 1, n_r))]
    for peer in peers:
        pl.semaphore_signal(barrier, inc=1, device_id=peer, device_id_type=MESH)
    pl.semaphore_wait(barrier, len(peers))

    def remote(src, dst, send, recv, peer):
        return pltpu.make_async_remote_copy(
            src_ref=src, dst_ref=dst, send_sem=send, recv_sem=recv, device_id=peer, device_id_type=MESH
        )

    own = tuple(bit[b] for b in reversed(range(n_bits)))
    gather[(t,) + own] = shard[...]
    ag_z = []
    for k in range(1, n_t):
        spot = gather.at[(t,) + own]
        ag_z.append(remote(spot, spot, ag_z_send.at[k - 1], ag_z_recv.at[k - 1], (lax.rem(t + k, n_t), r)))
        ag_z[-1].start()
    cot_in = pltpu.make_async_copy(cot_hbm, cot.at[pl.ds(0, F)], cot_sem)
    cot_in.start()

    def spread(values, f, row):
        col = lax.broadcasted_iota(jnp.int32, (W, C), 0)
        left = jnp.where(col == 0, 0.0, pltpu.roll(values, 1, 0))
        right = jnp.where(col == W - 1, 0.0, pltpu.roll(values, W - 1, 0))
        wide[f, row, :, 0:C] = left.astype(bf16)
        wide[f, row, :, C : 2 * C] = values.astype(bf16)
        wide[f, row, :, 2 * C : 3 * C] = right.astype(bf16)

    def act_row(f, h):
        normed, _ = normalize(video[f, h].astype(f32))
        act = normed * jax.nn.sigmoid(normed)
        spread(act, f, h + 1)
        act_t[f, :, pl.ds(pl.multiple_of(h * W, W), W)] = act.T.astype(bf16)

    def exchange(which):
        @pl.loop(0, F)
        def _(f):
            edge_out[2 * which, f] = wide[f, 1, :, C : 2 * C]
            edge_out[2 * which + 1, f] = wide[f, R, :, C : 2 * C]

        up = remote(
            edge_out.at[2 * which], edge_in.at[2 * which + 1],
            edge_send.at[2 * which], edge_recv.at[2 * which + 1], (t, r - 1),
        )
        down = remote(
            edge_out.at[2 * which + 1], edge_in.at[2 * which],
            edge_send.at[2 * which + 1], edge_recv.at[2 * which], (t, r + 1),
        )

        @pl.when(r > 0)
        def _():
            up.start()

        @pl.when(r < n_r - 1)
        def _():
            down.start()

        return up, down

    def receive(which, up, down):
        def fill(side, row):
            @pl.loop(0, F)
            def _(f):
                spread(edge_in[2 * which + side, f].astype(f32), f, row)

        def blank(row):
            @pl.loop(0, F)
            def _(f):
                wide[f, row] = jnp.zeros((W, 3 * C), bf16)

        @pl.when(r > 0)
        def _():
            up.wait_send()
            down.wait_recv()
            fill(0, 0)

        @pl.when(r == 0)
        def _():
            blank(0)

        @pl.when(r < n_r - 1)
        def _():
            down.wait_send()
            up.wait_recv()
            fill(1, R + 1)

        @pl.when(r == n_r - 1)
        def _():
            blank(R + 1)

    @pl.loop(0, F)
    def _(f):
        act_row(f, 0)
        act_row(f, R - 1)

    up_a, down_a = exchange(0)

    high = list(reversed(range(n_bits)))
    swapped = [high[1], high[0]] + high[2:] if n_bits >= 3 else high
    streams = [(high, 0), (swapped, half)]

    def ag_step(step):
        copies = []
        for s, (order, start) in enumerate(streams):
            done = order[:step]
            index = tuple(slice(None) if b in done else bit[b] for b in high)
            spot = gather.at[(slice(None),) + index + (pl.ds(start, half),)]
            b = order[step]
            copies.append(remote(spot, spot, ag_send.at[s, step], ag_recv.at[s, step], (t, partner[b])))
        for copy in copies:
            copy.start()
        return copies

    def finish(copies):
        for copy in copies:
            copy.wait()

    finish(ag_z)
    going = ag_step(0)
    ahead = remote(cot_hbm.at[pl.ds(0, 2)], cot.at[pl.ds(F, 2)], frame_send.at[0], frame_recv.at[0], (t - 1, r))

    @pl.when(t > 0)
    def _():
        ahead.start()

    @pl.loop(0, F * (R - 2))
    def _(i):
        act_row(lax.div(i, R - 2), lax.rem(i, R - 2) + 1)

    finish(going)
    going = ag_step(1) if n_bits > 1 else []
    receive(0, up_a, down_a)
    finish(going)
    for step in range(2, n_bits):
        finish(ag_step(step))

    for d in range(n_t * n_r):
        rr = d % n_r
        piece = gather[(d // n_r,) + tuple((rr >> b) & 1 for b in high)].astype(f32)
        acc_s[d * n_s : (d + 1) * n_s] = piece[:n_s]
        acc_t[d * n_tmp : (d + 1) * n_tmp] = piece[n_s : n_s + n_tmp]
    w_s[...] = acc_s[...].astype(bf16)
    w_t[...] = acc_t[...].astype(bf16)

    def forward(i):
        f = F - 1 - lax.div(i, per)
        h = lax.rem(i, per) * CH
        total = jnp.zeros((CH * W, C), f32)
        for ky in range(3):
            total += mm(wide[f, pl.ds(h + ky, CH)].reshape(CH * W, 3 * C), w_s[3 * C * ky : 3 * C * (ky + 1)])
        sigmoid = jax.nn.sigmoid(total)
        slope[f, pl.ds(h, CH)] = (sigmoid * (1.0 + total * (1.0 - sigmoid))).reshape(CH, W, C)
        hidden = total * sigmoid
        hid[f + 2, pl.ds(h, CH)] = hidden.astype(bf16).reshape(CH, W, C)
        hid_t[f, :, pl.ds(pl.multiple_of(h * W, W), CH * W)] = hidden.T.astype(bf16)

    pl.loop(0, 2 * per)(forward)
    past = remote(hid.at[pl.ds(F, 2)], hid.at[pl.ds(0, 2)], frame_send.at[1], frame_recv.at[1], (t + 1, r))

    @pl.when(t < n_t - 1)
    def _():
        past.start()

    pl.loop(2 * per, F * per)(forward)

    for i in range(3):
        for j in range(3):
            source = C * (3 * (2 - i) + 2 - j)
            wb_s[C * (3 * i + j) : C * (3 * i + j + 1)] = acc_s[source : source + C].T.astype(bf16)
        wb_t[C * i : C * (i + 1)] = acc_t[C * (2 - i) : C * (3 - i)].T.astype(bf16)

    cot_in.wait()

    @pl.when(t > 0)
    def _():
        ahead.wait_send()

    @pl.when(t < n_t - 1)
    def _():
        ahead.wait_recv()

    @pl.when(t == n_t - 1)
    def _():
        cot[F : F + 2] = jnp.zeros((2, R, W, C), bf16)

    def back(i):
        f = lax.div(i, per)
        h = lax.rem(i, per) * CH
        total = jnp.zeros((CH * W, C), f32)
        for m in range(3):
            total += mm(cot[f + m, pl.ds(h, CH)].reshape(CH * W, C), wb_t[C * m : C * (m + 1)])
        for k in range(CH):
            spread(total[k * W : (k + 1) * W] * slope[f, h + k], f, h + k + 1)

    pl.loop(0, F * per)(back)
    up_g, down_g = exchange(1)

    for k in range(3):
        acc_t[C * k : C * (k + 1)] = jnp.zeros((C, C), f32)

    @pl.loop(0, F)
    def _(f):
        for k in range(3):
            acc_t[C * k : C * (k + 1)] += mm(hid_t[f], cot[f + 2 - k].reshape(R * W, C))

    def mix(i):
        f = lax.div(i, per)
        h = lax.rem(i, per) * CH
        total = video[f, pl.ds(h, CH)].reshape(CH * W, C).astype(f32)
        for k in range(3):
            total += mm(hid[f + k, pl.ds(h, CH)].reshape(CH * W, C), w_t[C * k : C * (k + 1)])
        output[f, pl.ds(h, CH)] = total.astype(bf16).reshape(CH, W, C)

    pl.loop(2 * per, F * per)(mix)
    receive(1, up_g, down_g)

    acc_s[...] = jnp.zeros(acc_s.shape, f32)

    @pl.loop(0, F)
    def _(f):
        for i in range(3):
            found = mm(act_t[f], wide[f, pl.ds(i, R)].reshape(R * W, 3 * C))
            for j in range(3):
                block = C * (3 * (2 - i) + 2 - j)
                acc_s[block : block + C] += found[:, C * j : C * (j + 1)]

    for d in range(n_t * n_r):
        work[d, :n_s] = acc_s[d * n_s : (d + 1) * n_s]
        work[d, n_s : n_s + n_tmp] = acc_t[d * n_tmp : (d + 1) * n_tmp]
        if n_s + n_tmp < SH:
            work[d, n_s + n_tmp :] = jnp.zeros((SH - n_s - n_tmp, C), f32)

    offsets = []
    place = 0
    for b in range(n_bits):
        offsets.append(place)
        place += n_t * (1 << (n_bits - 1 - b))

    def slot(b, s, mine):
        count = 1 << (n_bits - 1 - b)
        tt, hi = lax.div(s, count), lax.rem(s, count)
        low = lax.rem(r, 1 << b)
        this = bit[b] if mine else 1 - bit[b]
        return tt * n_r + hi * (1 << (b + 1)) + this * (1 << b) + low

    def rs_start(b):
        count = n_t * (1 << (n_bits - 1 - b))

        @pl.loop(0, count)
        def _(s):
            rs_out[offsets[b] + s] = work[slot(b, s, False)].astype(bf16)

        span = pl.ds(offsets[b], count)
        copy = remote(rs_out.at[span], rs_in.at[span], rs_send.at[b], rs_recv.at[b], (t, partner[b]))
        copy.start()
        return copy

    def rs_finish(b, copy):
        copy.wait()

        @pl.loop(0, n_t * (1 << (n_bits - 1 - b)))
        def _(s):
            spot = slot(b, s, True)
            work[spot] = work[spot] + rs_in[offsets[b] + s].astype(f32)

    def data_back(i):
        f = lax.div(i, per)
        h = lax.rem(i, per) * CH
        total = jnp.zeros((CH * W, C), f32)
        for k in range(3):
            total += mm(wide[f, pl.ds(h + k, CH)].reshape(CH * W, 3 * C), wb_s[3 * C * k : 3 * C * (k + 1)])
        for k in range(CH):
            normed, inv_rms = normalize(video[f, h + k].astype(f32))
            grad_norm = total[k * W : (k + 1) * W] * silu_slope(normed)
            grad_in = inv_rms * (grad_norm - normed * jnp.mean(grad_norm * normed, axis=-1, keepdims=True))
            grad_video[f, h + k] = (cot[f, h + k].astype(f32) + grad_in).astype(bf16)

    chunks = F * per
    going = rs_start(0)
    for b in range(n_bits):
        pl.loop(b * chunks // n_bits, (b + 1) * chunks // n_bits)(data_back)
        rs_finish(b, going)
        if b + 1 < n_bits:
            going = rs_start(b + 1)

    z_copies = []
    for k in range(1, n_t):
        to = lax.rem(t + k, n_t)
        z_out[k - 1] = work[to * n_r + r].astype(bf16)
        z_copies.append(
            remote(z_out.at[k - 1], z_in.at[k - 1], z_send.at[k - 1], z_recv.at[k - 1], (to, r))
        )
        z_copies[-1].start()

    @pl.when(t < n_t - 1)
    def _():
        past.wait_send()

    @pl.when(t > 0)
    def _():
        past.wait_recv()

    @pl.when(t == 0)
    def _():
        hid[0:2] = jnp.zeros((2, R, W, C), bf16)

    pl.loop(0, 2 * per)(mix)

    finish(z_copies)
    total = work[t * n_r + r]
    for k in range(n_t - 1):
        total += z_in[k].astype(f32)
    grads[...] = total * factor


def shards(video, spatial_weight, temporal_weight, cotangent):
    _, F, R, W, C = video.shape
    n_t, n_r = lax.axis_size("tm"), lax.axis_size("rows")
    n_s, n_tmp = spatial_weight.shape[0], temporal_weight.shape[0]
    SH = -(-(n_s + n_tmp) // 32) * 32
    n_bits = n_r.bit_length() - 1
    total_cells = F * R * W * n_t * n_r
    factor = float(total_cells) ** (-0.5)
    parts = [spatial_weight, temporal_weight]
    if SH > n_s + n_tmp:
        parts.append(jnp.zeros((SH - n_s - n_tmp, C), bf16))
    shard = jnp.concatenate(parts, axis=0)
    dims = (n_t, n_r, F, R, W, C, n_s, n_tmp, factor)
    n_all = n_t * n_r
    rs_slots = n_t * (n_r - 1)
    dma = pltpu.SemaphoreType.DMA
    vmem = pl.BlockSpec(memory_space=pltpu.VMEM)
    output, grad_video, grads = pl.pallas_call(
        functools.partial(kernel, dims),
        out_shape=(
            jax.ShapeDtypeStruct((F, R, W, C), bf16),
            jax.ShapeDtypeStruct((F, R, W, C), bf16),
            jax.ShapeDtypeStruct((SH, C), f32),
        ),
        in_specs=[vmem, vmem, pl.BlockSpec(memory_space=pl.ANY)],
        out_specs=(vmem, vmem, vmem),
        scratch_shapes=[
            pltpu.VMEM((F, R + 2, W, 3 * C), bf16),
            pltpu.VMEM((F, C, R * W), bf16),
            pltpu.VMEM((F, R, W, C), f32),
            pltpu.VMEM((F + 2, R, W, C), bf16),
            pltpu.VMEM((F, C, R * W), bf16),
            pltpu.VMEM((F + 2, R, W, C), bf16),
            pltpu.VMEM((n_s * n_all, C), f32),
            pltpu.VMEM((n_tmp * n_all, C), f32),
            pltpu.VMEM((n_all, SH, C), f32),
            pltpu.VMEM((n_s * n_all, C), bf16),
            pltpu.VMEM((n_tmp * n_all, C), bf16),
            pltpu.VMEM((n_s * n_all, C), bf16),
            pltpu.VMEM((n_tmp * n_all, C), bf16),
            pltpu.VMEM((n_t,) + (2,) * n_bits + (SH, C), bf16),
            pltpu.VMEM((4, F, W, C), bf16),
            pltpu.VMEM((4, F, W, C), bf16),
            pltpu.VMEM((rs_slots, SH, C), bf16),
            pltpu.VMEM((rs_slots, SH, C), bf16),
            pltpu.VMEM((n_t - 1, SH, C), bf16),
            pltpu.VMEM((n_t - 1, SH, C), bf16),
            dma((n_t - 1,)), dma((n_t - 1,)),
            dma((2, n_bits)), dma((2, n_bits)),
            dma((4,)), dma((4,)),
            dma((2,)), dma((2,)),
            dma((n_bits,)), dma((n_bits,)),
            dma((n_t - 1,)), dma((n_t - 1,)),
            dma,
        ],
        compiler_params=pltpu.CompilerParams(
            collective_id=0, has_side_effects=True, vmem_limit_bytes=58 * 1024 * 1024
        ),
        cost_estimate=pl.CostEstimate(
            flops=24 * F * R * W * C * C * 3, bytes_accessed=F * R * W * C * 8, transcendentals=F * R * W * C * 3
        ),
    )(video[0], shard, cotangent[0])
    return (output[None], grad_video[None], grads[:n_s], grads[n_s : n_s + n_tmp])


def solution(mesh):
    in_specs = (
        P(None, "tm", "rows", None, None),
        P(("tm", "rows"), None),
        P(("tm", "rows"), None),
        P(None, "tm", "rows", None, None),
    )
    out_specs = (
        P(None, "tm", "rows", None, None),
        P(None, "tm", "rows", None, None),
        P(("tm", "rows"), None),
        P(("tm", "rows"), None),
    )
    return jax.shard_map(shards, mesh=mesh, in_specs=in_specs, out_specs=out_specs, check_vma=False)
```
